32 devices in a mesh: row: 8 (over y, x, core), col: 4 (over z).
Axes of the slice: x: 2, y: 2, z: 4, core: 2. Of those that a mesh axis runs over, the one named last changes fastest.
Arguments:
- amplitudes: bfloat16 [32, 32, 256, 256], P('row', 'col'), may hold values from -6 to 6
- coulomb: bfloat16 [32, 32, 256, 256], P('row', 'col'), may hold values from -12 to 12
- fit_ov: bfloat16 [1024, 32, 256], P(None, 'col'), may hold values from -0.25 to 0.25
- fit_vv: bfloat16 [16, 256, 256], P('row'), may hold values from -0.5 to 0.5
- eps_occ: float32 [32], replicated, may hold values from -2 to -0.5
- eps_vir: float32 [256], replicated, may hold values from 0.5 to 2.5
Outputs:
- updated: bfloat16 [32, 32, 256, 256], P('row', 'col')
The draws below stay inside these ranges and needn't reach their ends.
All inputs are finite; a program needn't handle non-finite values.
Results may differ from the reference program's by a relative error of at most 0.009.
Values may be sent and summed in bfloat16 or wider, within the bound.
No kernel may reach another device: no remote copies, remote signals or barrier semaphores. Data moves between devices by JAX's collectives and lax.ppermute only.
A program may use at most 128 MiB of HBM per device.

```python
import jax
import jax.numpy as jnp
from jax import lax

O = 32
V = 256
X = 1024
QL = 16
ITERS = 2


def levels(own_key, dims, split, least, high):
    def one(position, blocks):
        steps = jax.random.uniform(jax.random.fold_in(jax.random.fold_in(own_key, 6), position), (blocks,), jnp.float32, least / len(split), high / len(split))
        return jnp.repeat(jnp.exp(steps), dims[position] // blocks).reshape((-1,) + (1,) * (len(dims) - position - 1))

    gain = one(*split[0])
    for cut in split[1:]:
        gain = gain * one(*cut)
    return gain


def centred(own_key, shape, scale, limit, cuts=(), held_as=jnp.bfloat16):
    level = levels(own_key, shape, cuts, -0.22, 0.18) if cuts else 1.0
    array = jax.random.normal(own_key, shape, jnp.float32) * scale * level
    return jnp.minimum(jnp.maximum(array, -limit), limit).astype(held_as)


def setup_inputs(seed: int = 0) -> dict:
    key_list = jax.random.split(jax.random.key(seed), 7)
    amplitudes = centred(key_list[0], (O, O, V, V), 1.0, 6.0, ((0, 8), (1, 4)))
    coulomb = centred(key_list[1], (O, O, V, V), 2.0, 12.0, ((0, 8), (1, 4)))
    fit_ov = centred(key_list[2], (X, O, V), ((X * O * V) ** -0.25), 0.25, ((1, 4),))
    fit_vv = centred(key_list[3], (QL, V, V), ((QL * V * V) ** -0.25), 0.5, ((0, 8),))
    eps_occ = jnp.clip(jax.random.uniform(key_list[4], (O,), jnp.float32, -2.0, -0.5), -2.0, -0.5)
    eps_vir = jnp.clip(jax.random.uniform(key_list[5], (V,), jnp.float32, 0.5, 2.5), 0.5, 2.5)
    return dict(amplitudes=amplitudes, coulomb=coulomb, fit_ov=fit_ov, fit_vv=fit_vv, eps_occ=eps_occ, eps_vir=eps_vir)


def reference(amplitudes, coulomb, fit_ov, fit_vv, eps_occ, eps_vir):
    denominator = (eps_occ[:, None, None, None] + eps_occ[None, :, None, None]
                   - eps_vir[None, None, :, None] - eps_vir[None, None, None, :])
    current = amplitudes
    fit_wide = fit_ov.astype(jnp.float32)
    for sweep in range(ITERS):
        flattened = current.reshape(O * O, V, V).astype(jnp.float32)

        def add_auxiliary(running, fitting):
            fitting = fitting.astype(jnp.float32)
            contracted = jnp.einsum("ac,pcd->pad", fitting, flattened).astype(jnp.bfloat16)
            running = running + jnp.einsum("pad,bd->pab", contracted.astype(jnp.float32), fitting)
            return running, None

        initial = jnp.zeros((O * O, V, V), jnp.float32)
        ladder, unused = lax.scan(add_auxiliary, initial, fit_vv)
        ladder = ladder.reshape(O, O, V, V)
        cycle_partial = jnp.einsum("qkc,ikac->qia", fit_wide, current.astype(jnp.float32)).astype(jnp.bfloat16)
        cycle_term = jnp.einsum("qia,qjb->ijab", cycle_partial.astype(jnp.float32), fit_wide).astype(jnp.bfloat16)
        swapped = jnp.transpose(cycle_term, (1, 0, 3, 2))
        summed = coulomb.astype(jnp.float32) + ladder + cycle_term.astype(jnp.float32) + swapped.astype(jnp.float32)
        current = (summed / denominator).astype(jnp.bfloat16)
    return current
```

```python
import functools

import jax
import jax.numpy as jnp
from jax import lax
from jax.experimental import pallas as pl
from jax.experimental.pallas import tpu as pltpu
from jax.sharding import PartitionSpec as P

ITERS = 2
PLAN = ("P", "P", "P", "0", "P", "LLL", "0", "1", "LLL", "0", "1", "LL", "0", "1", "0", "1", "1")
BF16 = jnp.bfloat16
F32 = jnp.float32
MIB = 2**20
HBM = pltpu.HBM
NT = (((1,), (1,)), ((), ()))
ANY = pl.BlockSpec(memory_space=pl.ANY)
SMEM = pl.BlockSpec(memory_space=pltpu.SMEM)
CHEAP = pl.CostEstimate(flops=1, bytes_accessed=1, transcendentals=0)


def in_hbm(value):
    return pltpu.with_memory_space_constraint(value, HBM)


def in_vmem(value):
    return pltpu.with_memory_space_constraint(value, pltpu.VMEM)


def product(a, b):
    return jnp.dot(a, b, preferred_element_type=F32)


def product_turned(a, b):
    return lax.dot_general(a, b, NT, preferred_element_type=F32)


def ladder_kernel(n_after, first, *refs):
    t_ref, coulomb_ref, fit_ref = refs[:3]
    out_ref = refs[-1]
    batch, virtual, _ = fit_ref.shape
    left = jnp.concatenate(
        [product(fit_ref[q], t_ref[0]).astype(BF16) for q in range(batch)], axis=1
    )
    total = coulomb_ref[0].astype(F32)
    for q in range(batch):
        total += product_turned(left[:, q * virtual : (q + 1) * virtual], fit_ref[q])
    out_ref[0] = total


def ladder(current, coulomb, fit, base, first, pairs, after):
    total_pairs, virtual, _ = current.shape
    whole = lambda i: (0, 0, 0)
    block = pl.BlockSpec((1, virtual, virtual), lambda i: (first + i, 0, 0))
    extra = ([] if base is None else [in_hbm(base)]) + list(after)
    return pl.pallas_call(
        functools.partial(ladder_kernel, len(extra), first),
        grid=(pairs,),
        in_specs=[block, block, pl.BlockSpec(fit.shape, whole)] + [ANY] * len(extra),
        out_specs=block,
        out_shape=HBM((total_pairs, virtual, virtual), F32),
        input_output_aliases={} if base is None else {3: 0},
        compiler_params=pltpu.CompilerParams(vmem_limit_bytes=24 * MIB),
        cost_estimate=CHEAP,
        name="ladder",
    )(in_hbm(current), in_hbm(coulomb), in_vmem(fit), *extra)


def partial_kernel(info_ref, t_ref, fov_ref, *rest):
    out_ref = rest[-1]
    out_ref[...] = panel_sum(t_ref, fov_ref)


def panel_sum(t_ref, fov_ref):
    others, virtual, batch = fov_ref.shape
    rows = jnp.concatenate([t_ref[k] for k in range(others)], axis=1)
    return product(rows, fov_ref[...].reshape(others * virtual, batch)).astype(BF16)


def partial_sum(info, current, fov, after=()):
    others, virtual, batch = fov.shape
    return pl.pallas_call(
        partial_kernel,
        grid_spec=pltpu.PrefetchScalarGridSpec(
            num_scalar_prefetch=1,
            grid=(1,),
            in_specs=[
                pl.BlockSpec((others, virtual, virtual), lambda g, info: (info[0], 0, 0)),
                pl.BlockSpec(fov.shape, lambda g, info: (0, 0, 0)),
            ]
            + [ANY] * len(after),
            out_specs=pl.BlockSpec((virtual, batch), lambda g, info: (0, 0)),
        ),
        out_shape=jax.ShapeDtypeStruct((virtual, batch), BF16),
        compiler_params=pltpu.CompilerParams(vmem_limit_bytes=24 * MIB),
        cost_estimate=CHEAP,
        name="partial",
    )(info, in_hbm(current), in_vmem(fov), *after)


def finish_kernel(info_ref, occ_ref, base_ref, fov_ref, rows_ref, evr_ref, evc_ref, own_ref, *rest):
    others, virtual, batch = fov_ref.shape
    seen = rest[:others]
    tail = [r for r in rest[others:]]
    with_partial = info_ref.shape[0] > 0 and len(tail) > 0 and tail[-1].shape == own_ref.shape
    out_ref = tail[-2] if with_partial else tail[-1]
    i = info_ref[0]
    mine = own_ref[...]
    rows = rows_ref[0]
    n_rows = occ_ref.shape[0] - others
    for place in range(others):
        j = info_ref[1 + place]
        fov = fov_ref[j]
        value = base_ref[j]
        value += product_turned(mine, fov)
        value += product_turned(rows, seen[place][...])
        denominator = occ_ref[i] + occ_ref[n_rows + j] - evc_ref[...] - evr_ref[...]
        out_ref[j] = (value / denominator).astype(BF16)
    if with_partial:
        tail[-1][...] = panel_sum(out_ref, fov_ref)


def finish(info, occ, base, fov, rows, eps_vir, own, seen, into, with_partial, after):
    others, virtual, batch = fov.shape
    flat = lambda g, info: (0, 0)
    square = pl.BlockSpec((others, virtual, virtual), lambda g, info: (info[0], 0, 0))
    panel = pl.BlockSpec((virtual, batch), flat)
    outs, out_specs = [HBM(base.shape, BF16)], [square]
    if with_partial:
        outs.append(jax.ShapeDtypeStruct((virtual, batch), BF16))
        out_specs.append(panel)
    extra = ([] if into is None else [in_hbm(into)]) + list(after)
    return pl.pallas_call(
        finish_kernel,
        grid_spec=pltpu.PrefetchScalarGridSpec(
            num_scalar_prefetch=1,
            grid=(1,),
            in_specs=[
                SMEM,
                square,
                pl.BlockSpec(fov.shape, lambda g, info: (0, 0, 0)),
                pl.BlockSpec((1, virtual, batch), lambda g, info: (info[0], 0, 0)),
                pl.BlockSpec((1, virtual), flat),
                pl.BlockSpec((virtual, 1), flat),
                panel,
            ]
            + [panel] * len(seen)
            + [ANY] * len(extra),
            out_specs=out_specs,
        ),
        out_shape=outs,
        input_output_aliases={} if into is None else {8 + len(seen): 0},
        compiler_params=pltpu.CompilerParams(vmem_limit_bytes=28 * MIB),
        cost_estimate=CHEAP,
        name="finish",
    )(info, occ, in_hbm(base), in_vmem(fov), in_hbm(rows), eps_vir[None, :], eps_vir[:, None], own, *seen, *extra)


def merge_kernel(kind, flag_ref, *refs):
    out_ref = refs[-1]
    if kind == "take":
        out_ref[...] = refs[0][...]
    elif kind == "add":
        out_ref[...] = (refs[0][...].astype(F32) + refs[1][...].astype(F32)).astype(BF16)
    else:
        came = flag_ref[0] == 0

        @pl.when(came)
        def _():
            out_ref[...] = refs[1][...]

        @pl.when(jnp.logical_not(came))
        def _():
            out_ref[...] = refs[0][...]


def merge(kind, values, flag, after):
    value = values[0]
    whole = pl.BlockSpec(value.shape, lambda g: (0, 0))
    return pl.pallas_call(
        functools.partial(merge_kernel, kind),
        grid=(1,),
        in_specs=[SMEM] + [whole] * len(values) + [ANY] * len(after),
        out_specs=whole,
        out_shape=jax.ShapeDtypeStruct(value.shape, value.dtype),
        compiler_params=pltpu.CompilerParams(vmem_limit_bytes=6 * MIB),
        cost_estimate=CHEAP,
        name="merge",
    )(flag, *values, *after)


def keep_kernel(value_ref, out_ref):
    out_ref[...] = value_ref[...]


def kept_in_vmem(value):
    whole = pl.BlockSpec((1, *value.shape[1:]), lambda g: (g, 0, 0))
    return pl.pallas_call(
        keep_kernel,
        grid=(value.shape[0],),
        in_specs=[whole],
        out_specs=whole,
        out_shape=pltpu.VMEM(value.shape, value.dtype),
        compiler_params=pltpu.CompilerParams(vmem_limit_bytes=8 * MIB),
        cost_estimate=CHEAP,
        name="keep",
    )(value)


def swap(value, axis, size, bit):
    return lax.ppermute(value, axis, [(k, k ^ bit) for k in range(size)])


def spread_steps(rows, columns):
    group = rows // columns
    bits = [1 << b for b in range(columns.bit_length() - 1)]
    row = lax.axis_index("row")
    lane = row % group
    away = (row // group) ^ lax.axis_index("col")
    steps = []
    for step in range(len(bits)):
        pairs = []
        has = jnp.zeros((), jnp.bool_)
        for m in range(group):
            order = bits[m % len(bits) :] + bits[: m % len(bits)]
            reached = {0}
            for bit in order[:step]:
                reached |= {g ^ bit for g in reached}
            pairs += [
                (((g ^ c) * group + m) * columns + c, ((g ^ order[step] ^ c) * group + m) * columns + c)
                for c in range(columns)
                for g in sorted(reached)
            ]
            has = has | ((lane == m) & ((away & sum(order[step:])) == 0))
        steps.append((pairs, has.astype(jnp.int32)[None]))
    return steps


def gather_rows(fit_ov, rows):
    part = fit_ov.shape[0] // rows
    piece = lax.dynamic_slice_in_dim(fit_ov, lax.axis_index("row") * part, part, axis=0)
    every = lax.all_gather(piece, "col", axis=1, tiled=True)
    mine = lax.all_to_all(every, "row", split_axis=1, concat_axis=0, tiled=True)
    return jnp.transpose(mine, (1, 2, 0))


def body(rows, columns, amplitudes, coulomb, fit_ov, fit_vv, eps_occ, eps_vir):
    occ_local, occ_other, virtual, _ = amplitudes.shape
    group = rows // columns
    row, col = lax.axis_index("row"), lax.axis_index("col")
    low = col % 2
    occ = jnp.concatenate(
        [
            lax.dynamic_slice_in_dim(eps_occ, row * occ_local, occ_local),
            lax.dynamic_slice_in_dim(eps_occ, col * occ_other, occ_other),
        ]
    )
    pairs = occ_local * occ_other
    chunks = occ_local // 2
    keeps = [2 * c + low for c in range(chunks)]
    sends = [2 * c + 1 - low for c in range(chunks)]
    lanes = [(row % group) ^ x for x in range(group)]
    slots = [
        lane * occ_local + index for lane in lanes for c in range(chunks) for index in (keeps[c], sends[c])
    ]

    def info(index):
        return jnp.stack([index, *slots]).astype(jnp.int32)

    fit = kept_in_vmem(lax.all_gather(fit_vv, "row", axis=0, tiled=True))
    fov = kept_in_vmem(jnp.transpose(fit_ov, (1, 2, 0)))
    mine = gather_rows(fit_ov, rows)
    current = amplitudes.reshape(pairs, virtual, virtual)
    flat_coulomb = coulomb.reshape(pairs, virtual, virtual)
    steps = spread_steps(rows, columns)
    none = jnp.zeros((1,), jnp.int32)
    order = []

    def run(kernel, *args):
        got = kernel(*args, order[-1:])
        order.append(got[0] if isinstance(got, (list, tuple)) else got)
        return got

    def travel(made, out):
        value = made[1]
        bit = 1
        while bit < columns:
            moving = swap(made[0] if bit == 1 else value, "col", columns, bit)
            value = run(merge, "add", [value, moving], none)
            bit *= 2
            if bit < columns:
                yield
        out["kept"] = value
        moving = swap(value, "col", columns, 1)
        ways, came = {"kept": value}, {"kept": lax.ppermute(value, ("row", "col"), steps[0][0])}
        for stage in range(len(steps) + 1):
            yield
            for name, now in (("kept", stage), ("sent", stage - 1)):
                if not 0 <= now < len(steps):
                    continue
                ways[name] = run(merge, "pick", [ways[name], came[name]], steps[now][1])
                if now + 1 < len(steps):
                    came[name] = lax.ppermute(ways[name], ("row", "col"), steps[now + 1][0])
                else:
                    out["seen", name] = [ways[name]] + [
                        swap(ways[name], "row", rows, lane) for lane in range(1, group)
                    ]
            if stage == 0:
                out["sent"] = ways["sent"] = run(merge, "take", [moving], none)
                came["sent"] = lax.ppermute(ways["sent"], ("row", "col"), steps[0][0])

    wanted = [index for c in range(chunks) for index in (sends[c], keeps[c])]
    outs = None
    for sweep in range(ITERS + 1):
        made = [[] for _ in range(chunks)]
        before = outs
        if sweep > 0:
            seen = [
                before[c]["seen", name][lane]
                for lane in range(group)
                for c in range(chunks)
                for name in ("kept", "sent")
            ]
        into = None

        def make(place):
            nonlocal into
            c = place // 2
            if sweep == 0:
                token = [fit] if place == len(wanted) - 1 else []
                got = partial_sum(info(wanted[place]), current, fov, order[-1:] + token)
                order.append(got)
                made[c].append(got)
                return
            own = before[c]["kept" if place % 2 else "sent"]
            last = sweep == ITERS
            got = finish(
                info(wanted[place]), occ, base, fov, mine, eps_vir, own, seen, into, not last, order[-1:] if into is None else []
            )
            into = got[0]
            if not last:
                order.append(got[1])
                made[c].append(got[1])

        if sweep == ITERS:
            for place in range(len(wanted)):
                make(place)
            return into.reshape(amplitudes.shape)
        outs = [{} for _ in range(chunks)]
        travels = [travel(made[c], outs[c]) for c in range(chunks)]
        if chunks == 2 and columns == 4:
            plan = PLAN
        else:
            plan = ["P"] * len(wanted) + ["LLLLLLLL"]
        size = pairs // 8
        place = piece = 0
        next_base = None
        for what in plan:
            if what == "P":
                make(place)
                place += 1
            elif what[0] == "L":
                source = current if sweep == 0 else into
                count = len(what) * size
                next_base = ladder(source, flat_coulomb, fit, next_base, piece, count, order[-1:])
                order.append(in_hbm(next_base))
                piece += count
            else:
                next(travels[int(what)], None)
        for rest in travels:
            list(rest)
        base = next_base


def solution(mesh):
    in_specs = (
        P("row", "col", None, None),
        P("row", "col", None, None),
        P(None, "col", None),
        P("row", None, None),
        P(),
        P(),
    )
    out_specs = P("row", "col", None, None)
    local = functools.partial(body, mesh.shape["row"], mesh.shape["col"])
    return jax.shard_map(local, mesh=mesh, in_specs=in_specs, out_specs=out_specs, check_vma=False)
```

```python
import functools

import jax
import jax.numpy as jnp
from jax import lax
from jax.experimental import pallas as pl
from jax.experimental.pallas import tpu as pltpu
from jax.sharding import PartitionSpec as P

ITERS = 2
PLAN = ("P", "P", "P", "0", "P", "LLL", "0", "1", "LLL", "0", "1", "LL", "0", "1", "0", "1", "1")
BF16 = jnp.bfloat16
F32 = jnp.float32
MIB = 2**20
HBM = pltpu.HBM
NT = (((1,), (1,)), ((), ()))
ANY = pl.BlockSpec(memory_space=pl.ANY)
SMEM = pl.BlockSpec(memory_space=pltpu.SMEM)
CHEAP = pl.CostEstimate(flops=1, bytes_accessed=1, transcendentals=0)


def in_hbm(value):
    return pltpu.with_memory_space_constraint(value, HBM)


def in_vmem(value):
    return pltpu.with_memory_space_constraint(value, pltpu.VMEM)


def product(a, b):
    return jnp.dot(a, b, preferred_element_type=F32)


def product_turned(a, b):
    return lax.dot_general(a, b, NT, preferred_element_type=F32)


def ladder_kernel(n_after, first, *refs):
    t_ref, coulomb_ref, fit_ref = refs[:3]
    out_ref = refs[-1]
    batch, virtual, _ = fit_ref.shape
    left = jnp.concatenate(
        [product(fit_ref[q], t_ref[0]).astype(BF16) for q in range(batch)], axis=1
    )
    total = coulomb_ref[0].astype(F32)
    for q in range(batch):
        total += product_turned(left[:, q * virtual : (q + 1) * virtual], fit_ref[q])
    out_ref[0] = total


def ladder(current, coulomb, fit, base, first, pairs, after):
    total_pairs, virtual, _ = current.shape
    whole = lambda i: (0, 0, 0)
    block = pl.BlockSpec((1, virtual, virtual), lambda i: (first + i, 0, 0))
    extra = ([] if base is None else [in_hbm(base)]) + list(after)
    return pl.pallas_call(
        functools.partial(ladder_kernel, len(extra), first),
        grid=(pairs,),
        in_specs=[block, block, pl.BlockSpec(fit.shape, whole)] + [ANY] * len(extra),
        out_specs=block,
        out_shape=HBM((total_pairs, virtual, virtual), F32),
        input_output_aliases={} if base is None else {3: 0},
        compiler_params=pltpu.CompilerParams(vmem_limit_bytes=24 * MIB),
        cost_estimate=CHEAP,
        name="ladder",
    )(in_hbm(current), in_hbm(coulomb), in_vmem(fit), *extra)


def partial_kernel(info_ref, t_ref, fov_ref, *rest):
    out_ref = rest[-1]
    out_ref[...] = panel_sum(t_ref, fov_ref)


def panel_sum(t_ref, fov_ref):
    others, virtual, batch = fov_ref.shape
    rows = jnp.concatenate([t_ref[k] for k in range(others)], axis=1)
    return product(rows, fov_ref[...].reshape(others * virtual, batch)).astype(BF16)


def partial_sum(info, current, fov, after=()):
    others, virtual, batch = fov.shape
    return pl.pallas_call(
        partial_kernel,
        grid_spec=pltpu.PrefetchScalarGridSpec(
            num_scalar_prefetch=1,
            grid=(1,),
            in_specs=[
                pl.BlockSpec((others, virtual, virtual), lambda g, info: (info[0], 0, 0)),
                pl.BlockSpec(fov.shape, lambda g, info: (0, 0, 0)),
            ]
            + [ANY] * len(after),
            out_specs=pl.BlockSpec((virtual, batch), lambda g, info: (0, 0)),
        ),
        out_shape=jax.ShapeDtypeStruct((virtual, batch), BF16),
        compiler_params=pltpu.CompilerParams(vmem_limit_bytes=24 * MIB),
        cost_estimate=CHEAP,
        name="partial",
    )(info, in_hbm(current), in_vmem(fov), *after)


def finish_kernel(info_ref, occ_ref, base_ref, fov_ref, rows_ref, evr_ref, evc_ref, own_ref, *rest):
    others, virtual, batch = fov_ref.shape
    seen = rest[:others]
    tail = [r for r in rest[others:]]
    with_partial = info_ref.shape[0] > 0 and len(tail) > 0 and tail[-1].shape == own_ref.shape
    out_ref = tail[-2] if with_partial else tail[-1]
    i = info_ref[0]
    mine = own_ref[...]
    rows = rows_ref[0]
    n_rows = occ_ref.shape[0] - others
    for place in range(others):
        j = info_ref[1 + place]
        fov = fov_ref[j]
        value = base_ref[j]
        value += product_turned(mine, fov)
        value += product_turned(rows, seen[place][...])
        denominator = occ_ref[i] + occ_ref[n_rows + j] - evc_ref[...] - evr_ref[...]
        out_ref[j] = (value / denominator).astype(BF16)
    if with_partial:
        tail[-1][...] = panel_sum(out_ref, fov_ref)


def finish(info, occ, base, fov, rows, eps_vir, own, seen, into, with_partial, after):
    others, virtual, batch = fov.shape
    flat = lambda g, info: (0, 0)
    square = pl.BlockSpec((others, virtual, virtual), lambda g, info: (info[0], 0, 0))
    panel = pl.BlockSpec((virtual, batch), flat)
    outs, out_specs = [HBM(base.shape, BF16)], [square]
    if with_partial:
        outs.append(jax.ShapeDtypeStruct((virtual, batch), BF16))
        out_specs.append(panel)
    extra = ([] if into is None else [in_hbm(into)]) + list(after)
    return pl.pallas_call(
        finish_kernel,
        grid_spec=pltpu.PrefetchScalarGridSpec(
            num_scalar_prefetch=1,
            grid=(1,),
            in_specs=[
                SMEM,
                square,
                pl.BlockSpec(fov.shape, lambda g, info: (0, 0, 0)),
                pl.BlockSpec((1, virtual, batch), lambda g, info: (info[0], 0, 0)),
                pl.BlockSpec((1, virtual), flat),
                pl.BlockSpec((virtual, 1), flat),
                panel,
            ]
            + [panel] * len(seen)
            + [ANY] * len(extra),
            out_specs=out_specs,
        ),
        out_shape=outs,
        input_output_aliases={} if into is None else {8 + len(seen): 0},
        compiler_params=pltpu.CompilerParams(vmem_limit_bytes=28 * MIB),
        cost_estimate=CHEAP,
        name="finish",
    )(info, occ, in_hbm(base), in_vmem(fov), in_hbm(rows), eps_vir[None, :], eps_vir[:, None], own, *seen, *extra)


def finish_all_kernel(count, with_partial, n_extra, info_ref, occ_ref, base_ref, rows_ref, evr_ref, evc_ref, fov_ref, *rest):
    own, rest = rest[:count], rest[count:]
    mine = rest[-1]
    others = fov_ref.shape[0]
    seen = rest[:others]
    outs = rest[others + n_extra : -1]
    out_ref = outs[0]
    step = pl.program_id(0)
    i = info_ref[step]
    n_rows = occ_ref.shape[0] - others
    for n in range(count):

        @pl.when(step == n)
        def _():
            mine[...] = own[n][...]

    for place in range(others):
        j = info_ref[count + place]
        value = base_ref[j]
        value += product_turned(mine[...], fov_ref[j])
        value += product_turned(rows_ref[0], seen[place][...])
        denominator = occ_ref[i] + occ_ref[n_rows + j] - evc_ref[...] - evr_ref[...]
        out_ref[j] = (value / denominator).astype(BF16)
    if with_partial:
        total = panel_sum(out_ref, fov_ref)
        for n in range(count):

            @pl.when(step == n)
            def _():
                outs[1 + n][...] = total


def finish_all(indices, slots, occ, base, fov, rows, eps_vir, own, seen, into, with_partial, after):
    others, virtual, batch = fov.shape
    count = len(indices)
    flat = lambda g, info: (0, 0)
    once = pl.Buffered(1)
    square = pl.BlockSpec((others, virtual, virtual), lambda g, info: (info[g], 0, 0))
    outs, out_specs = [HBM(base.shape, BF16)], [square]
    if with_partial:
        outs += [jax.ShapeDtypeStruct((virtual, batch), BF16)] * count
        out_specs += [pl.BlockSpec((virtual, batch), flat)] * count
    extra = ([] if into is None else [in_hbm(into)]) + list(after)
    return pl.pallas_call(
        functools.partial(finish_all_kernel, count, with_partial, len(extra)),
        grid_spec=pltpu.PrefetchScalarGridSpec(
            num_scalar_prefetch=1,
            grid=(count,),
            in_specs=[
                SMEM,
                square,
                pl.BlockSpec((1, virtual, batch), lambda g, info: (info[g], 0, 0)),
                pl.BlockSpec((1, virtual), flat),
                pl.BlockSpec((virtual, 1), flat),
            ]
            + [pl.BlockSpec(fov.shape, lambda g, info: (0, 0, 0), pipeline_mode=once)]
            + [pl.BlockSpec((virtual, batch), flat, pipeline_mode=once)] * (count + len(seen))
            + [ANY] * len(extra),
            out_specs=out_specs,
            scratch_shapes=[pltpu.VMEM((virtual, batch), BF16)],
        ),
        out_shape=outs,
        input_output_aliases={} if into is None else {7 + count + len(seen): 0},
        compiler_params=pltpu.CompilerParams(vmem_limit_bytes=32 * MIB),
        cost_estimate=CHEAP,
        name="finish_all",
    )(
        jnp.stack([*indices, *slots]).astype(jnp.int32),
        occ,
        in_hbm(base),
        in_hbm(rows),
        eps_vir[None, :],
        eps_vir[:, None],
        in_hbm(fov),
        *own,
        *seen,
        *extra,
    )


def merge_kernel(kind, flag_ref, *refs):
    out_ref = refs[-1]
    if kind == "take":
        out_ref[...] = refs[0][...]
    elif kind == "add":
        out_ref[...] = (refs[0][...].astype(F32) + refs[1][...].astype(F32)).astype(BF16)
    else:
        came = flag_ref[0] == 0

        @pl.when(came)
        def _():
            out_ref[...] = refs[1][...]

        @pl.when(jnp.logical_not(came))
        def _():
            out_ref[...] = refs[0][...]


def merge(kind, values, flag, after):
    value = values[0]
    whole = pl.BlockSpec(value.shape, lambda g: (0, 0))
    return pl.pallas_call(
        functools.partial(merge_kernel, kind),
        grid=(1,),
        in_specs=[SMEM] + [whole] * len(values) + [ANY] * len(after),
        out_specs=whole,
        out_shape=jax.ShapeDtypeStruct(value.shape, value.dtype),
        compiler_params=pltpu.CompilerParams(vmem_limit_bytes=6 * MIB),
        cost_estimate=CHEAP,
        name="merge",
    )(flag, *values, *after)


def keep_kernel(value_ref, out_ref):
    out_ref[...] = value_ref[...]


def kept_in_vmem(value):
    whole = pl.BlockSpec((1, *value.shape[1:]), lambda g: (g, 0, 0))
    return pl.pallas_call(
        keep_kernel,
        grid=(value.shape[0],),
        in_specs=[whole],
        out_specs=whole,
        out_shape=pltpu.VMEM(value.shape, value.dtype),
        compiler_params=pltpu.CompilerParams(vmem_limit_bytes=8 * MIB),
        cost_estimate=CHEAP,
        name="keep",
    )(value)


def swap(value, axis, size, bit):
    return lax.ppermute(value, axis, [(k, k ^ bit) for k in range(size)])


def spread_steps(rows, columns):
    group = rows // columns
    bits = [1 << b for b in range(columns.bit_length() - 1)]
    row = lax.axis_index("row")
    lane = row % group
    away = (row // group) ^ lax.axis_index("col")
    steps = []
    for step in range(len(bits)):
        pairs = []
        has = jnp.zeros((), jnp.bool_)
        for m in range(group):
            order = bits[m % len(bits) :] + bits[: m % len(bits)]
            reached = {0}
            for bit in order[:step]:
                reached |= {g ^ bit for g in reached}
            pairs += [
                (((g ^ c) * group + m) * columns + c, ((g ^ order[step] ^ c) * group + m) * columns + c)
                for c in range(columns)
                for g in sorted(reached)
            ]
            has = has | ((lane == m) & ((away & sum(order[step:])) == 0))
        steps.append((pairs, has.astype(jnp.int32)[None]))
    return steps


def gather_rows(fit_ov, rows):
    part = fit_ov.shape[0] // rows
    piece = lax.dynamic_slice_in_dim(fit_ov, lax.axis_index("row") * part, part, axis=0)
    every = lax.all_gather(piece, "col", axis=1, tiled=True)
    mine = lax.all_to_all(every, "row", split_axis=1, concat_axis=0, tiled=True)
    return jnp.transpose(mine, (1, 2, 0))


def body(rows, columns, amplitudes, coulomb, fit_ov, fit_vv, eps_occ, eps_vir):
    occ_local, occ_other, virtual, _ = amplitudes.shape
    group = rows // columns
    row, col = lax.axis_index("row"), lax.axis_index("col")
    low = col % 2
    occ = jnp.concatenate(
        [
            lax.dynamic_slice_in_dim(eps_occ, row * occ_local, occ_local),
            lax.dynamic_slice_in_dim(eps_occ, col * occ_other, occ_other),
        ]
    )
    pairs = occ_local * occ_other
    chunks = occ_local // 2
    keeps = [2 * c + low for c in range(chunks)]
    sends = [2 * c + 1 - low for c in range(chunks)]
    lanes = [(row % group) ^ x for x in range(group)]
    slots = [
        lane * occ_local + index for lane in lanes for c in range(chunks) for index in (keeps[c], sends[c])
    ]

    def info(index):
        return jnp.stack([index, *slots]).astype(jnp.int32)

    fit = kept_in_vmem(lax.all_gather(fit_vv, "row", axis=0, tiled=True))
    plain_fov = jnp.transpose(fit_ov, (1, 2, 0))
    fov = kept_in_vmem(plain_fov)
    mine = gather_rows(fit_ov, rows)
    current = amplitudes.reshape(pairs, virtual, virtual)
    flat_coulomb = coulomb.reshape(pairs, virtual, virtual)
    steps = spread_steps(rows, columns)
    none = jnp.zeros((1,), jnp.int32)
    order = []

    def run(kernel, *args):
        got = kernel(*args, order[-1:])
        order.append(got[0] if isinstance(got, (list, tuple)) else got)
        return got

    def travel(made, out):
        value = made[1]
        bit = 1
        while bit < columns:
            moving = swap(made[0] if bit == 1 else value, "col", columns, bit)
            value = run(merge, "add", [value, moving], none)
            bit *= 2
            if bit < columns:
                yield
        out["kept"] = value
        moving = swap(value, "col", columns, 1)
        ways, came = {"kept": value}, {"kept": lax.ppermute(value, ("row", "col"), steps[0][0])}
        for stage in range(len(steps) + 1):
            yield
            for name, now in (("kept", stage), ("sent", stage - 1)):
                if not 0 <= now < len(steps):
                    continue
                ways[name] = run(merge, "pick", [ways[name], came[name]], steps[now][1])
                if now + 1 < len(steps):
                    came[name] = lax.ppermute(ways[name], ("row", "col"), steps[now + 1][0])
                else:
                    out["seen", name] = [ways[name]] + [
                        swap(ways[name], "row", rows, lane) for lane in range(1, group)
                    ]
            if stage == 0:
                out["sent"] = ways["sent"] = run(merge, "take", [moving], none)
                came["sent"] = lax.ppermute(ways["sent"], ("row", "col"), steps[0][0])

    wanted = [index for c in range(chunks) for index in (sends[c], keeps[c])]
    outs = None
    for sweep in range(ITERS + 1):
        made = [[] for _ in range(chunks)]
        before = outs
        if sweep > 0:
            seen = [
                before[c]["seen", name][lane]
                for lane in range(group)
                for c in range(chunks)
                for name in ("kept", "sent")
            ]
        into = None

        def make(place):
            nonlocal into
            c = place // 2
            if sweep == 0:
                token = [fit] if place == len(wanted) - 1 else []
                got = partial_sum(info(wanted[place]), current, fov, order[-1:] + token)
                order.append(got)
                made[c].append(got)
                return
            own = before[c]["kept" if place % 2 else "sent"]
            last = sweep == ITERS
            got = finish(
                info(wanted[place]), occ, base, fov, mine, eps_vir, own, seen, into, not last, order[-1:] if into is None else []
            )
            into = got[0]
            if not last:
                order.append(got[1])
                made[c].append(got[1])

        if sweep == ITERS:
            own = [before[c][name] for c in range(chunks) for name in ("sent", "kept")]
            into = finish_all(
                wanted, slots, occ, base, plain_fov, mine, eps_vir, own, seen, None, False, []
            )[0]
            return into.reshape(amplitudes.shape)
        outs = [{} for _ in range(chunks)]
        travels = [travel(made[c], outs[c]) for c in range(chunks)]
        if chunks == 2 and columns == 4:
            plan = PLAN
        else:
            plan = ["P"] * len(wanted) + ["LLLLLLLL"]
        size = pairs // 8
        place = piece = 0
        next_base = None
        for what in plan:
            if what == "P":
                make(place)
                place += 1
            elif what[0] == "L":
                source = current if sweep == 0 else into
                count = len(what) * size
                next_base = ladder(source, flat_coulomb, fit, next_base, piece, count, order[-1:])
                order.append(in_hbm(next_base))
                piece += count
            else:
                next(travels[int(what)], None)
        for rest in travels:
            list(rest)
        base = next_base


def solution(mesh):
    in_specs = (
        P("row", "col", None, None),
        P("row", "col", None, None),
        P(None, "col", None),
        P("row", None, None),
        P(),
        P(),
    )
    out_specs = P("row", "col", None, None)
    local = functools.partial(body, mesh.shape["row"], mesh.shape["col"])
    return jax.shard_map(local, mesh=mesh, in_specs=in_specs, out_specs=out_specs, check_vma=False)
```
